32 devices in a mesh: dp: 8 (over z, x), ctx: 4 (over y, core).
Axes of the slice: x: 2, y: 2, z: 4, core: 2. Of those that a mesh axis runs over, the one named last changes fastest.
Arguments:
- inputs: bfloat16 [4, 8, 512, 960], P(None, 'dp', 'ctx'), may hold values from -6 to 6
- positions: int32 [4, 8, 512], P(None, 'dp', 'ctx'), may hold values from 0 to 511, as said below
- cotangent: bfloat16 [4, 8, 512, 960], P(None, 'dp', 'ctx'), may hold values from -6 to 6
- attn_gain: bfloat16 [960], P('dp'), may hold values from 0.099609375 to 1.8984375
- w_query: bfloat16 [960, 960], P('dp', 'ctx'), may hold values from -0.1875 to 0.1875
- w_key: bfloat16 [960, 320], P('dp', 'ctx'), may hold values from -0.1875 to 0.1875
- w_value: bfloat16 [960, 320], P('dp', 'ctx'), may hold values from -0.1875 to 0.1875
- w_output: bfloat16 [960, 960], P('dp', 'ctx'), may hold values from -0.75 to 0.75
- ffn_gain: bfloat16 [960], P('dp'), may hold values from 0.099609375 to 1.8984375
- w_gate: bfloat16 [960, 2560], P('dp', 'ctx'), may hold values from -0.1875 to 0.1875
- w_up: bfloat16 [960, 2560], P('dp', 'ctx'), may hold values from -0.1875 to 0.1875
- w_down: bfloat16 [2560, 960], P('dp', 'ctx'), may hold values from -0.25 to 0.25
Outputs:
- outputs: bfloat16 [4, 8, 512, 960], P(None, 'dp', 'ctx')
- input_grad: float32 [4, 8, 512, 960], P(None, 'dp', 'ctx')
- attn_gain_grad: float32 [960], P('dp')
- w_query_grad: float32 [960, 960], P('dp', 'ctx')
- w_key_grad: float32 [960, 320], P('dp', 'ctx')
- w_value_grad: float32 [960, 320], P('dp', 'ctx')
- w_output_grad: float32 [960, 960], P('dp', 'ctx')
- ffn_gain_grad: float32 [960], P('dp')
- w_gate_grad: float32 [960, 2560], P('dp', 'ctx')
- w_up_grad: float32 [960, 2560], P('dp', 'ctx')
- w_down_grad: float32 [2560, 960], P('dp', 'ctx')
The draws below stay inside these ranges and needn't reach their ends.
Inputs may be any that keep to these rules, and one draw needn't show every extreme that they name: Within a sequence, positions rise by one from token to token inside a document and restart at 0 where a new document begins; the first document of a sequence may have begun before it. In each micro-batch, of the 1 sequence that one index of dp holds, one has a first document that ends after token 448 and whose last position is 511.
All inputs are finite; a program needn't handle non-finite values.
Results may differ from the reference program's by a relative error of at most 0.02.
Values may be sent and summed in bfloat16 or wider, within the bound.
A program may use at most 192 MiB of HBM per device.

```python
import math
import jax
import jax.numpy as jnp
from jax import lax

D = 960
HEADS = 15
KV_HEADS = 5
HEAD_DIM = 64
FF = 2560
MICRO = 4
SEQ_GRP = 1
SEQ_PART = 128
SEQ = 512
NSEQ = 8
KVW = 320


def draw_positions(key, part):
    key = jax.random.fold_in(key, 7)
    start_key, chosen_key, offset_key, break_key = jax.random.split(key, 4)
    group_count = NSEQ // SEQ_GRP
    start_marks = jax.random.randint(start_key, (MICRO, NSEQ, SEQ), 0, max(2, SEQ // 2)) == 0
    chosen = jnp.repeat(jax.random.randint(chosen_key, (MICRO, group_count), 0, SEQ_GRP), SEQ_GRP, axis=1)
    member = jnp.arange(NSEQ, dtype=jnp.int32) % SEQ_GRP
    long_doc = (member[None, :] == chosen)[:, :, None]
    token_index = jnp.arange(SEQ, dtype=jnp.int32)
    first_break = jax.random.randint(break_key, (MICRO, NSEQ, 1), SEQ - SEQ_PART // 2 + 1, SEQ + 1)
    opened_long = start_marks & (token_index > first_break) | (token_index == first_break)
    opened_other = start_marks & (token_index > 0)
    opened = jnp.where(long_doc, opened_long, opened_other)
    first_open = jnp.min(jnp.where(opened, token_index, SEQ), axis=2, keepdims=True)
    offset = jax.random.randint(offset_key, (MICRO, NSEQ, 1), 0, SEQ - first_open + 1)
    offset = jnp.where(long_doc, SEQ - first_break, offset)
    latest = lax.cummax(jnp.where(opened, token_index, 0), axis=2)
    return jnp.where(latest > 0, token_index - latest, token_index + offset).astype(jnp.int32)


def block_levels(rng, shape, cuts, least, high):
    factor_of, own = 1.0, jax.random.fold_in(rng, 6)
    for position, shards_of in cuts:
        heights = jnp.exp(jax.random.uniform(jax.random.fold_in(own, position), (shards_of,), jnp.float32, least / len(cuts), high / len(cuts)))
        factor_of = factor_of * jnp.repeat(heights, shape[position] // shards_of).reshape([-1 if axis == position else 1 for axis in range(len(shape))])
    return factor_of


def noise(key, extent, scale, bound, cuts=(), held_as=jnp.bfloat16):
    drawn = scale * jax.random.normal(key, extent, jnp.float32)
    if cuts:
        drawn = drawn * block_levels(key, extent, cuts, -0.22, 0.18)
    return jnp.clip(drawn, -bound, bound).astype(held_as)


def setup_inputs(seed: int = 0) -> dict:
    seeds = jax.random.split(jax.random.key(seed), 13)
    inputs = noise(seeds[0], (MICRO, NSEQ, SEQ, D), 1.0, 6.0, ((1, 8), (2, 4)))
    positions = draw_positions(jax.random.fold_in(seeds[12], 71), 0)
    cotangent = noise(seeds[2], (MICRO, NSEQ, SEQ, D), 1.0, 6.0, ((1, 8), (2, 4)))
    attn_gain = jnp.clip(1.0 + 0.18 * jax.random.normal(seeds[3], (D,), jnp.float32), 0.099609375, 1.8984375).astype(jnp.bfloat16)
    w_query = noise(seeds[4], (D, D), D ** -0.5, 0.1875, ((0, 8), (1, 4)))
    w_key = noise(seeds[5], (D, KVW), D ** -0.5, 0.1875, ((0, 8), (1, 4)))
    w_value = noise(seeds[6], (D, KVW), D ** -0.5, 0.1875, ((0, 8), (1, 4)))
    w_output = noise(seeds[7], (D, D), (D // 16) ** -0.5, 0.75, ((0, 8), (1, 4)))
    ffn_gain = jnp.clip(1.0 + 0.18 * jax.random.normal(seeds[8], (D,), jnp.float32), 0.099609375, 1.8984375).astype(jnp.bfloat16)
    w_gate = noise(seeds[9], (D, FF), D ** -0.5, 0.1875, ((0, 8), (1, 4)))
    w_up = noise(seeds[10], (D, FF), D ** -0.5, 0.1875, ((0, 8), (1, 4)))
    w_down = noise(seeds[11], (FF, D), (FF // 4) ** -0.5, 0.25, ((0, 8), (1, 4)))
    return dict(inputs=inputs, positions=positions, cotangent=cotangent, attn_gain=attn_gain, w_query=w_query, w_key=w_key, w_value=w_value, w_output=w_output, ffn_gain=ffn_gain, w_gate=w_gate, w_up=w_up, w_down=w_down)


EPS = 1e-05
HIGHEST_PRECISION = lax.Precision.HIGHEST

@jax.custom_vjp
def low(v):
    return lax.optimization_barrier(v.astype(jnp.bfloat16)).astype(jnp.float32)

@jax.custom_vjp
def low_back(v):
    return v

def low_keep(v):
    return (low(v), None)

def low_pass(kept, grad):
    return (grad,)

def back_keep(v):
    return (v, None)

def back_low(kept, grad):
    return (low(grad),)
low.defvjp(low_keep, low_pass)
low_back.defvjp(back_keep, back_low)

def turn_tables(places, head_width):
    half_width = head_width // 2
    frequency = 10000.0 ** (-(jnp.arange(half_width, dtype=jnp.float32) * (2.0 / head_width)))
    angles = places.astype(jnp.float32)[..., None] * frequency
    return (jnp.cos(angles)[..., None, :], jnp.sin(angles)[..., None, :])

def rotate(vectors, cosine, sine_part):
    half_width = vectors.shape[-1] // 2
    first_half = vectors[..., :half_width]
    second_half = vectors[..., half_width:]
    return jnp.concatenate([first_half * cosine - second_half * sine_part, second_half * cosine + first_half * sine_part], axis=-1)

def matmul(left, right):
    return jnp.dot(left, right, precision=HIGHEST_PRECISION)

def attention(queries, keys_low, values_low, starts):
    seq_count, length = starts.shape
    group_size = HEADS // KV_HEADS
    score_scale = HEAD_DIM ** (-0.5)
    query_heads = queries.reshape(seq_count, length, KV_HEADS, group_size, HEAD_DIM)
    scores = jnp.einsum('gikhd,gjkd->gkhij', query_heads, keys_low, precision=HIGHEST_PRECISION) * score_scale
    scores = low_back(scores)
    key_index = jnp.arange(length, dtype=jnp.int32)
    allowed = (key_index[None, None, :] <= key_index[None, :, None]) & (key_index[None, None, :] >= starts[:, :, None])
    scores = jnp.where(allowed[:, None, None], scores, -1e+30)
    row_max = lax.optimization_barrier(jnp.max(scores, -1, keepdims=True))
    exponent = jnp.exp(scores - row_max)
    soft_weights = low(exponent / lax.optimization_barrier(jnp.sum(exponent, -1, keepdims=True)))
    attended = jnp.einsum('gkhij,gjkd->gikhd', soft_weights, values_low, precision=HIGHEST_PRECISION)
    return attended.reshape(seq_count, length, HEADS * HEAD_DIM)

def layer_block(params, activations, places):
    attn_gain, w_query, w_key, w_value, w_output, ffn_gain, w_gate, w_up, w_down = params
    seq_count, length = places.shape
    first_scale = lax.rsqrt(lax.optimization_barrier(jnp.mean(activations * activations, -1, keepdims=True)) + EPS)
    normed = low(activations * first_scale * attn_gain)
    cosine, sine_part = turn_tables(places, HEAD_DIM)
    query_pre = low_back(matmul(normed, w_query)).reshape(seq_count, length, HEADS, HEAD_DIM)
    key_pre = low_back(matmul(normed, w_key)).reshape(seq_count, length, KV_HEADS, HEAD_DIM)
    values_low = low(low_back(matmul(normed, w_value))).reshape(seq_count, length, KV_HEADS, HEAD_DIM)
    queries = low(rotate(query_pre, cosine, sine_part))
    keys_low = low(rotate(key_pre, cosine, sine_part))
    starts = jnp.arange(length, dtype=jnp.int32)[None, :] - places
    attended = low(low_back(attention(queries, keys_low, values_low, starts)))
    middle = activations + low_back(matmul(attended, w_output))
    second_scale = lax.rsqrt(lax.optimization_barrier(jnp.mean(middle * middle, -1, keepdims=True)) + EPS)
    normed2 = low(middle * second_scale * ffn_gain)
    gate_pre = low_back(matmul(normed2, w_gate))
    up_pre = low_back(matmul(normed2, w_up))
    hidden = low(jax.nn.silu(gate_pre) * up_pre)
    return middle + low_back(matmul(hidden, w_down))

def reference(inputs, positions, cotangent, attn_gain, w_query, w_key, w_value, w_output, ffn_gain, w_gate, w_up, w_down):
    params = tuple((weight.astype(jnp.float32) for weight in (attn_gain, w_query, w_key, w_value, w_output, ffn_gain, w_gate, w_up, w_down)))
    seq_total = MICRO * NSEQ
    group_size = math.gcd(seq_total, max(1, 4096 // SEQ))
    group_count = seq_total // group_size
    activations = inputs.astype(jnp.float32).reshape(group_count, group_size, SEQ, D)
    places = positions.reshape(group_count, group_size, SEQ)
    incoming = cotangent.astype(jnp.float32).reshape(group_count, group_size, SEQ, D)

    def one_group(summed, item):
        group_acts, group_places, group_cot = item

        def apply_block(weights, values_in):
            return layer_block(weights, values_in, group_places)
        result, pullback = jax.vjp(apply_block, params, group_acts)
        param_grads, input_grads = pullback(group_cot)
        summed = jax.tree.map(jnp.add, summed, param_grads)
        return (summed, (result, input_grads))
    zeros = tuple((jnp.zeros_like(weight) for weight in params))
    summed, (results, input_grads) = lax.scan(one_group, zeros, (activations, places, incoming))
    outputs = results.reshape(MICRO, NSEQ, SEQ, D).astype(jnp.bfloat16)
    input_grad = input_grads.reshape(MICRO, NSEQ, SEQ, D)
    return (outputs, input_grad, summed[0], summed[1], summed[2], summed[3], summed[4], summed[5], summed[6], summed[7], summed[8])
```

```python
import jax
import jax.numpy as jnp
from jax import lax
from jax.sharding import PartitionSpec as P

HEADS = 15
KV_HEADS = 5
HEAD_DIM = 64


EPS = 1e-05


def turn_tables(places, head_width):
    half_width = head_width // 2
    frequency = 10000.0 ** (-(jnp.arange(half_width, dtype=jnp.float32) * (2.0 / head_width)))
    angles = places.astype(jnp.float32)[..., None] * frequency
    return (jnp.cos(angles)[..., None, :], jnp.sin(angles)[..., None, :])


def rotate(vectors, cosine, sine_part):
    half_width = vectors.shape[-1] // 2
    first_half = vectors[..., :half_width]
    second_half = vectors[..., half_width:]
    return jnp.concatenate(
        [
            first_half * cosine - second_half * sine_part,
            second_half * cosine + first_half * sine_part,
        ],
        axis=-1,
    )


def unrotate(vectors, cosine, sine_part):
    half_width = vectors.shape[-1] // 2
    first_half = vectors[..., :half_width]
    second_half = vectors[..., half_width:]
    return jnp.concatenate(
        [
            first_half * cosine + second_half * sine_part,
            second_half * cosine - first_half * sine_part,
        ],
        axis=-1,
    )


def matmul(left, right):
    return jnp.dot(left, right, preferred_element_type=jnp.float32)


def flatten(values_in):
    return values_in.reshape(-1, values_in.shape[-1])


def swap(value, axis, bit):
    count = lax.axis_size(axis)
    return lax.ppermute(value, axis, [(i, i ^ bit) for i in range(count)])


def bits_of(count):
    bits, bit = [], 1
    while bit < count:
        bits.append(bit)
        bit *= 2
    return bits


def in_order(pieces, own, order):
    stacked = jnp.stack(pieces)
    places = [0] * len(order)
    for place, distance in enumerate(order):
        places[distance] = place
    table = jnp.array(places, jnp.int32)
    return [
        lax.dynamic_index_in_dim(stacked, table[own ^ i], 0, keepdims=False)
        for i in range(len(order))
    ]


def gather_rows(shard, own):
    order = [0]
    held = shard[None]
    for bit in reversed(bits_of(lax.axis_size("dp"))):
        held = jnp.concatenate([held, swap(held, "dp", bit)], 0)
        order = order + [distance ^ bit for distance in order]
    places = [0] * len(order)
    for place, distance in enumerate(order):
        places[distance] = place
    table = jnp.array(places, jnp.int32)
    return jnp.concatenate(
        [
            lax.dynamic_index_in_dim(held, table[own ^ i], 0, keepdims=False)
            for i in range(len(order))
        ],
        0,
    )


def gather_blocks(block, own):
    order, held = [0], [block]
    for bit in reversed(bits_of(lax.axis_size("ctx"))):
        held = held + [swap(piece, "ctx", bit) for piece in held]
        order = order + [distance ^ bit for distance in order]
    return in_order(held, own, order)


def block_grads(left, rights, own, ctx_count):
    blocks = []
    for right in rights:
        flat = flatten(right)
        width = flat.shape[1] // ctx_count
        blocks.append([flat[:, i * width : (i + 1) * width] for i in range(ctx_count)])
    stacked = jnp.stack([jnp.concatenate(parts, 1) for parts in zip(*blocks)])
    rows = flatten(left).T
    return [
        matmul(rows, lax.dynamic_index_in_dim(stacked, own ^ j, 0, keepdims=False)).astype(
            jnp.bfloat16
        )
        for j in range(ctx_count)
    ]


def add(left, right):
    return left.astype(jnp.float32) + right.astype(jnp.float32)


def scatter_sum(blocks, own_dp, wire):
    for bit in bits_of(lax.axis_size("ctx")):
        kept = blocks[0::2]
        arrived = [swap(block.astype(wire), "ctx", bit) for block in blocks[1::2]]
        blocks = [add(left, right) for left, right in zip(kept, arrived)]
    return scatter_rows(blocks[0], own_dp, wire)


def scatter_rows(total, own_dp, wire):
    count = lax.axis_size("dp")
    bits = bits_of(count)
    order = [0]
    for bit in reversed(bits):
        order = order + [distance ^ bit for distance in order]
    by_owner = total.reshape(count, total.shape[0] // count, *total.shape[1:]).astype(wire)
    held = jnp.stack(
        [lax.dynamic_index_in_dim(by_owner, own_dp ^ k, 0, keepdims=False) for k in order]
    )
    for bit in bits:
        half = held.shape[0] // 2
        arrived = swap(held[half:].astype(wire), "dp", bit)
        held = add(held[:half], arrived)
    return held[0]


def to_sequences(parts, own):
    count = lax.axis_size("ctx")
    pieces = [lax.dynamic_index_in_dim(parts, own ^ j, 0, keepdims=False) for j in range(count)]
    got = [pieces[0]] + [swap(pieces[j], "ctx", j) for j in range(1, count)]
    return jnp.concatenate(in_order(got, own, list(range(count))), 1)


def from_sequences(whole, own):
    count = lax.axis_size("ctx")
    part = whole.shape[1] // count
    pieces = [
        lax.dynamic_slice_in_dim(whole, (own ^ j) * part, part, 1) for j in range(count)
    ]
    got = [pieces[0]] + [swap(pieces[j], "ctx", j) for j in range(1, count)]
    return jnp.stack(in_order(got, own, list(range(count))))


def forward(weights, tokens, places):
    attn_gain, w_query, w_key, w_value, w_output, ffn_gain, w_gate, w_up, w_down = weights
    seq_count, part_len, model_width = tokens.shape
    group_size = HEADS // KV_HEADS
    score_scale = HEAD_DIM ** (-0.5)
    residual = tokens.astype(jnp.float32)
    first_scale = lax.rsqrt(jnp.mean(residual * residual, -1, keepdims=True) + EPS)
    normed = (residual * first_scale * attn_gain.astype(jnp.float32)).astype(jnp.bfloat16)
    cosine, sine_part = turn_tables(places, HEAD_DIM)
    queries = rotate(
        matmul(normed, w_query).reshape(seq_count, part_len, HEADS, HEAD_DIM), cosine, sine_part
    ).astype(jnp.bfloat16)
    keys_low = rotate(
        matmul(normed, w_key).reshape(seq_count, part_len, KV_HEADS, HEAD_DIM), cosine, sine_part
    ).astype(jnp.bfloat16)
    keys_low = keys_low.reshape(seq_count, part_len, KV_HEADS * HEAD_DIM)
    values_low = matmul(normed, w_value).astype(jnp.bfloat16)
    all_keys, all_values = keys_low, values_low
    length = all_keys.shape[1]
    key_heads = all_keys.reshape(seq_count, length, KV_HEADS, HEAD_DIM)
    value_heads = all_values.reshape(seq_count, length, KV_HEADS, HEAD_DIM)
    query_heads = queries.reshape(seq_count, part_len, KV_HEADS, group_size, HEAD_DIM)
    scores = (
        jnp.einsum("bikhd,bjkd->bkhij", query_heads, key_heads, preferred_element_type=jnp.float32)
        * score_scale
    )
    row_index = jnp.arange(part_len, dtype=jnp.int32)
    starts = row_index[None, :] - places
    col_index = jnp.arange(length, dtype=jnp.int32)
    allowed = (col_index[None, None, :] <= row_index[None, :, None]) & (
        col_index[None, None, :] >= starts[:, :, None]
    )
    scores = jnp.where(allowed[:, None, None], scores, -1e30)
    row_max = jnp.max(scores, -1, keepdims=True)
    exponent = jnp.exp(scores - row_max)
    soft_weights = exponent / jnp.sum(exponent, -1, keepdims=True)
    weights_low = soft_weights.astype(jnp.bfloat16)
    attended = jnp.einsum(
        "bkhij,bjkd->bikhd", weights_low, value_heads, preferred_element_type=jnp.float32
    )
    attended = attended.reshape(seq_count, part_len, model_width).astype(jnp.bfloat16)
    middle = residual + matmul(attended, w_output)
    second_scale = lax.rsqrt(jnp.mean(middle * middle, -1, keepdims=True) + EPS)
    normed2 = (middle * second_scale * ffn_gain.astype(jnp.float32)).astype(jnp.bfloat16)
    gate_pre = matmul(normed2, w_gate)
    up_pre = matmul(normed2, w_up)
    logistic = jax.nn.sigmoid(gate_pre)
    hidden_local = (gate_pre * logistic * up_pre).astype(jnp.bfloat16)
    result = (middle + matmul(hidden_local, w_down)).astype(jnp.bfloat16)
    stored = (
        residual,
        first_scale,
        normed,
        cosine,
        sine_part,
        query_heads,
        key_heads,
        value_heads,
        soft_weights,
        weights_low,
        attended,
        middle,
        second_scale,
        normed2,
        gate_pre,
        up_pre,
        logistic,
        hidden_local,
    )
    return (result, stored)


def backward(weights, stored, grad_low, own, ctx_count):
    attn_gain, w_query, w_key, w_value, w_output, ffn_gain, w_gate, w_up, w_down = weights
    (
        residual,
        first_scale,
        normed,
        cosine,
        sine_part,
        query_heads,
        key_heads,
        value_heads,
        soft_weights,
        weights_low,
        attended,
        middle,
        second_scale,
        ffn_input,
        gate_pre,
        up_pre,
        logistic,
        hidden,
    ) = stored
    seq_count, part_len, model_width = residual.shape
    length = key_heads.shape[1]
    kv_width = KV_HEADS * HEAD_DIM
    group_size = HEADS // KV_HEADS
    score_scale = HEAD_DIM ** (-0.5)
    grad_top = grad_low.astype(jnp.float32)
    grad_down = block_grads(hidden, [grad_low], own, ctx_count)
    grad_hidden_rows = matmul(grad_low, w_down.T)
    grad_up_low = (grad_hidden_rows * gate_pre * logistic).astype(jnp.bfloat16)
    grad_gate_low = (
        grad_hidden_rows * up_pre * (logistic * (1.0 + gate_pre * (1.0 - logistic)))
    ).astype(jnp.bfloat16)
    grad_gate = block_grads(ffn_input, [grad_gate_low], own, ctx_count)
    grad_upw = block_grads(ffn_input, [grad_up_low], own, ctx_count)
    grad_normed_terms = matmul(grad_gate_low, w_gate.T) + matmul(grad_up_low, w_up.T)
    grad_ffn = jnp.sum(flatten(grad_normed_terms * middle * second_scale), 0)
    weighted2 = ffn_gain.astype(jnp.float32) * grad_normed_terms
    grad_middle = (
        grad_top
        + second_scale * weighted2
        - middle * second_scale**3 * jnp.mean(weighted2 * middle, -1, keepdims=True)
    )
    branch_low = grad_middle.astype(jnp.bfloat16)
    grad_output = block_grads(attended, [branch_low], own, ctx_count)
    grad_attended = matmul(branch_low, w_output.T).astype(jnp.bfloat16)
    grad_heads = grad_attended.reshape(seq_count, part_len, KV_HEADS, group_size, HEAD_DIM)
    grad_probs = jnp.einsum(
        "bikhd,bjkd->bkhij", grad_heads, value_heads, preferred_element_type=jnp.float32
    )
    grad_scores = (
        soft_weights * (grad_probs - jnp.sum(soft_weights * grad_probs, -1, keepdims=True))
    ).astype(jnp.bfloat16)
    grad_queries = (
        jnp.einsum("bkhij,bjkd->bikhd", grad_scores, key_heads, preferred_element_type=jnp.float32)
        * score_scale
    )
    grad_keys = (
        jnp.einsum(
            "bkhij,bikhd->bjkd", grad_scores, query_heads, preferred_element_type=jnp.float32
        )
        * score_scale
    )
    grad_values = jnp.einsum(
        "bkhij,bikhd->bjkd", weights_low, grad_heads, preferred_element_type=jnp.float32
    )
    own_keys = grad_keys
    own_values = grad_values.reshape(seq_count, length, kv_width)
    query_low = (
        unrotate(grad_queries.reshape(seq_count, part_len, HEADS, HEAD_DIM), cosine, sine_part)
        .reshape(seq_count, part_len, model_width)
        .astype(jnp.bfloat16)
    )
    key_low = (
        unrotate(own_keys.reshape(seq_count, part_len, KV_HEADS, HEAD_DIM), cosine, sine_part)
        .reshape(seq_count, part_len, kv_width)
        .astype(jnp.bfloat16)
    )
    value_low = own_values.astype(jnp.bfloat16)
    grad_qkv = block_grads(normed, [query_low, key_low, value_low], own, ctx_count)
    grad_normed = (
        matmul(query_low, w_query.T) + matmul(key_low, w_key.T) + matmul(value_low, w_value.T)
    )
    grad_attn = jnp.sum(flatten(grad_normed * residual * first_scale), 0)
    weighted1 = attn_gain.astype(jnp.float32) * grad_normed
    grad_input = (
        grad_middle
        + first_scale * weighted1
        - residual * first_scale**3 * jnp.mean(weighted1 * residual, -1, keepdims=True)
    )
    return (
        grad_input,
        (
            grad_attn,
            grad_qkv,
            grad_output,
            grad_ffn,
            grad_gate,
            grad_upw,
            grad_down,
        ),
    )


def body(
    inputs,
    positions,
    cotangent,
    attn_gain,
    w_query,
    w_key,
    w_value,
    w_output,
    ffn_gain,
    w_gate,
    w_up,
    w_down,
):
    own = lax.axis_index("ctx")
    own_dp = lax.axis_index("dp")
    ctx_count = lax.axis_size("ctx")
    assert inputs.shape[0] == ctx_count
    q_width, k_width, o_width = w_query.shape[1], w_key.shape[1], w_output.shape[1]

    attn_pack = jnp.concatenate([w_query, w_key, w_value, w_output], 1)
    gains = gather_rows(jnp.stack([attn_gain, ffn_gain], 1), own_dp)
    tokens = to_sequences(inputs, own)
    places = to_sequences(positions, own)
    attn_blocks = gather_blocks(gather_rows(attn_pack, own_dp), own)
    gate_blocks = gather_blocks(gather_rows(w_gate, own_dp), own)
    up_blocks = gather_blocks(gather_rows(w_up, own_dp), own)
    down_blocks = gather_blocks(gather_rows(w_down, own_dp), own)
    grad_low = to_sequences(cotangent, own)

    def columns(start, width):
        return jnp.concatenate([block[:, start : start + width] for block in attn_blocks], 1)

    weights = (
        gains[:, 0],
        columns(0, q_width),
        columns(q_width, k_width),
        columns(q_width + k_width, k_width),
        columns(q_width + 2 * k_width, o_width),
        gains[:, 1],
        jnp.concatenate(gate_blocks, 1),
        jnp.concatenate(up_blocks, 1),
        jnp.concatenate(down_blocks, 1),
    )
    result, stored = forward(weights, tokens, places)
    outputs = from_sequences(result, own)
    grad_input, terms = backward(weights, stored, grad_low, own, ctx_count)
    grad_attn, grad_qkv, grad_output, grad_ffn, grad_gate, grad_up, grad_down = terms
    low = jnp.bfloat16
    down_owned = scatter_sum(grad_down, own_dp, low)
    gate_owned = scatter_sum(grad_gate, own_dp, low)
    up_owned = scatter_sum(grad_up, own_dp, low)
    output_owned = scatter_sum(grad_output, own_dp, low)
    qkv_owned = scatter_sum(grad_qkv, own_dp, low)
    gain_terms = jnp.stack([grad_attn, grad_ffn], 1)
    for bit in bits_of(ctx_count):
        gain_terms = gain_terms + swap(gain_terms, "ctx", bit)
    gain_owned = scatter_rows(gain_terms, own_dp, jnp.float32)
    input_grad = from_sequences(grad_input.astype(low), own).astype(jnp.float32)
    return (
        outputs,
        input_grad,
        gain_owned[:, 0],
        qkv_owned[:, :q_width],
        qkv_owned[:, q_width : q_width + k_width],
        qkv_owned[:, q_width + k_width :],
        output_owned,
        gain_owned[:, 1],
        gate_owned,
        up_owned,
        down_owned,
    )


def solution(mesh):
    return jax.shard_map(
        body,
        mesh=mesh,
        in_specs=(
            P(None, "dp", "ctx", None),
            P(None, "dp", "ctx"),
            P(None, "dp", "ctx", None),
            P("dp"),
            P("dp", "ctx"),
            P("dp", "ctx"),
            P("dp", "ctx"),
            P("dp", "ctx"),
            P("dp"),
            P("dp", "ctx"),
            P("dp", "ctx"),
            P("dp", "ctx"),
        ),
        out_specs=(
            P(None, "dp", "ctx", None),
            P(None, "dp", "ctx", None),
            P("dp"),
            P("dp", "ctx"),
            P("dp", "ctx"),
            P("dp", "ctx"),
            P("dp", "ctx"),
            P("dp"),
            P("dp", "ctx"),
            P("dp", "ctx"),
            P("dp", "ctx"),
        ),
        check_vma=False,
    )
```

```python
import jax
import jax.numpy as jnp
from jax import lax
from jax.sharding import PartitionSpec as P

HEADS = 15
KV_HEADS = 5
HEAD_DIM = 64


EPS = 1e-05


def turn_tables(places, head_width):
    half_width = head_width // 2
    frequency = 10000.0 ** (-(jnp.arange(half_width, dtype=jnp.float32) * (2.0 / head_width)))
    angles = places.astype(jnp.float32)[..., None] * frequency
    return (jnp.cos(angles)[..., None, :], jnp.sin(angles)[..., None, :])


def rotate(vectors, cosine, sine_part):
    half_width = vectors.shape[-1] // 2
    first_half = vectors[..., :half_width]
    second_half = vectors[..., half_width:]
    return jnp.concatenate(
        [
            first_half * cosine - second_half * sine_part,
            second_half * cosine + first_half * sine_part,
        ],
        axis=-1,
    )


def unrotate(vectors, cosine, sine_part):
    half_width = vectors.shape[-1] // 2
    first_half = vectors[..., :half_width]
    second_half = vectors[..., half_width:]
    return jnp.concatenate(
        [
            first_half * cosine + second_half * sine_part,
            second_half * cosine - first_half * sine_part,
        ],
        axis=-1,
    )


def matmul(left, right):
    return jnp.dot(left, right, preferred_element_type=jnp.float32)


def flatten(values_in):
    return values_in.reshape(-1, values_in.shape[-1])


def swap(value, axis, bit):
    count = lax.axis_size(axis)
    return lax.ppermute(value, axis, [(i, i ^ bit) for i in range(count)])


def tie(value, *earlier):
    return lax.optimization_barrier((value, earlier))[0]


def bits_of(count):
    bits, bit = [], 1
    while bit < count:
        bits.append(bit)
        bit *= 2
    return bits


def in_order(pieces, own, order):
    stacked = jnp.stack(pieces)
    places = [0] * len(order)
    for place, distance in enumerate(order):
        places[distance] = place
    table = jnp.array(places, jnp.int32)
    return [
        lax.dynamic_index_in_dim(stacked, table[own ^ i], 0, keepdims=False)
        for i in range(len(order))
    ]


def gather_rows(shard, own):
    order = [0]
    held = shard[None]
    first = None
    for bit in reversed(bits_of(lax.axis_size("dp"))):
        held = jnp.concatenate([held, swap(held, "dp", bit)], 0)
        first = held if first is None else first
        order = order + [distance ^ bit for distance in order]
    places = [0] * len(order)
    for place, distance in enumerate(order):
        places[distance] = place
    table = jnp.array(places, jnp.int32)
    return jnp.concatenate(
        [
            lax.dynamic_index_in_dim(held, table[own ^ i], 0, keepdims=False)
            for i in range(len(order))
        ],
        0,
    ), first


def gather_blocks(block, own):
    order, held = [0], [block]
    for bit in reversed(bits_of(lax.axis_size("ctx"))):
        held = held + [swap(piece, "ctx", bit) for piece in held]
        order = order + [distance ^ bit for distance in order]
    return in_order(held, own, order), held[1]


def block_grads(left, rights, own, ctx_count):
    blocks = []
    for right in rights:
        flat = flatten(right)
        width = flat.shape[1] // ctx_count
        blocks.append([flat[:, i * width : (i + 1) * width] for i in range(ctx_count)])
    stacked = jnp.stack([jnp.concatenate(parts, 1) for parts in zip(*blocks)])
    rows = flatten(left).T
    return [
        matmul(rows, lax.dynamic_index_in_dim(stacked, own ^ j, 0, keepdims=False)).astype(
            jnp.bfloat16
        )
        for j in range(ctx_count)
    ]


def add(left, right):
    return left.astype(jnp.float32) + right.astype(jnp.float32)


def fold(blocks, bit):
    arrived = [swap(block, "ctx", bit) for block in blocks[1::2]]
    return [
        add(left, right).astype(jnp.bfloat16) for left, right in zip(blocks[0::2], arrived)
    ]


def fold_rest(blocks):
    count = lax.axis_size("ctx")
    bit = count // len(blocks)
    while bit < count:
        blocks = fold(blocks, bit)
        bit *= 2
    return blocks[0]


def scatter_rows(total, own_dp, wire):
    count = lax.axis_size("dp")
    bits = bits_of(count)
    order = [0]
    for bit in reversed(bits):
        order = order + [distance ^ bit for distance in order]
    by_owner = total.reshape(count, total.shape[0] // count, *total.shape[1:]).astype(wire)
    held = jnp.stack(
        [lax.dynamic_index_in_dim(by_owner, own_dp ^ k, 0, keepdims=False) for k in order]
    )
    for bit in bits:
        half = held.shape[0] // 2
        arrived = swap(held[half:].astype(wire), "dp", bit)
        held = add(held[:half], arrived)
    return held[0]


def to_sequences(parts, own):
    count = lax.axis_size("ctx")
    pieces = [lax.dynamic_index_in_dim(parts, own ^ j, 0, keepdims=False) for j in range(count)]
    got = [pieces[0]] + [swap(pieces[j], "ctx", j) for j in range(1, count)]
    return jnp.concatenate(in_order(got, own, list(range(count))), 1)


def from_sequences(whole, own):
    count = lax.axis_size("ctx")
    part = whole.shape[1] // count
    pieces = [
        lax.dynamic_slice_in_dim(whole, (own ^ j) * part, part, 1) for j in range(count)
    ]
    got = [pieces[0]] + [swap(pieces[j], "ctx", j) for j in range(1, count)]
    return jnp.stack(in_order(got, own, list(range(count))))


def forward(weights, tokens, places):
    attn_gain, w_query, w_key, w_value, w_output, ffn_gain, w_gate, w_up, w_down = weights
    seq_count, part_len, model_width = tokens.shape
    group_size = HEADS // KV_HEADS
    score_scale = HEAD_DIM ** (-0.5)
    residual = tokens.astype(jnp.float32)
    first_scale = lax.rsqrt(jnp.mean(residual * residual, -1, keepdims=True) + EPS)
    normed = (residual * first_scale * attn_gain.astype(jnp.float32)).astype(jnp.bfloat16)
    cosine, sine_part = turn_tables(places, HEAD_DIM)
    queries = rotate(
        matmul(normed, w_query).reshape(seq_count, part_len, HEADS, HEAD_DIM), cosine, sine_part
    ).astype(jnp.bfloat16)
    keys_low = rotate(
        matmul(normed, w_key).reshape(seq_count, part_len, KV_HEADS, HEAD_DIM), cosine, sine_part
    ).astype(jnp.bfloat16)
    keys_low = keys_low.reshape(seq_count, part_len, KV_HEADS * HEAD_DIM)
    values_low = matmul(normed, w_value).astype(jnp.bfloat16)
    all_keys, all_values = keys_low, values_low
    length = all_keys.shape[1]
    key_heads = all_keys.reshape(seq_count, length, KV_HEADS, HEAD_DIM)
    value_heads = all_values.reshape(seq_count, length, KV_HEADS, HEAD_DIM)
    query_heads = queries.reshape(seq_count, part_len, KV_HEADS, group_size, HEAD_DIM)
    scores = (
        jnp.einsum("bikhd,bjkd->bkhij", query_heads, key_heads, preferred_element_type=jnp.float32)
        * score_scale
    )
    row_index = jnp.arange(part_len, dtype=jnp.int32)
    starts = row_index[None, :] - places
    col_index = jnp.arange(length, dtype=jnp.int32)
    allowed = (col_index[None, None, :] <= row_index[None, :, None]) & (
        col_index[None, None, :] >= starts[:, :, None]
    )
    scores = jnp.where(allowed[:, None, None], scores, -1e30)
    row_max = jnp.max(scores, -1, keepdims=True)
    exponent = jnp.exp(scores - row_max)
    soft_weights = exponent / jnp.sum(exponent, -1, keepdims=True)
    weights_low = soft_weights.astype(jnp.bfloat16)
    attended = jnp.einsum(
        "bkhij,bjkd->bikhd", weights_low, value_heads, preferred_element_type=jnp.float32
    )
    attended = attended.reshape(seq_count, part_len, model_width).astype(jnp.bfloat16)
    middle = residual + matmul(attended, w_output)
    second_scale = lax.rsqrt(jnp.mean(middle * middle, -1, keepdims=True) + EPS)
    normed2 = (middle * second_scale * ffn_gain.astype(jnp.float32)).astype(jnp.bfloat16)
    gate_pre = matmul(normed2, w_gate)
    up_pre = matmul(normed2, w_up)
    logistic = jax.nn.sigmoid(gate_pre)
    hidden_local = (gate_pre * logistic * up_pre).astype(jnp.bfloat16)
    result = (middle + matmul(hidden_local, w_down)).astype(jnp.bfloat16)
    stored = (
        residual,
        first_scale,
        normed,
        cosine,
        sine_part,
        query_heads,
        key_heads,
        value_heads,
        soft_weights,
        weights_low,
        attended,
        middle,
        second_scale,
        normed2,
        gate_pre,
        up_pre,
        logistic,
        hidden_local,
    )
    return (result, stored)


def backward(weights, stored, grad_low, own, ctx_count):
    attn_gain, w_query, w_key, w_value, w_output, ffn_gain, w_gate, w_up, w_down = weights
    (
        residual,
        first_scale,
        normed,
        cosine,
        sine_part,
        query_heads,
        key_heads,
        value_heads,
        soft_weights,
        weights_low,
        attended,
        middle,
        second_scale,
        ffn_input,
        gate_pre,
        up_pre,
        logistic,
        hidden,
    ) = stored
    seq_count, part_len, model_width = residual.shape
    length = key_heads.shape[1]
    kv_width = KV_HEADS * HEAD_DIM
    group_size = HEADS // KV_HEADS
    score_scale = HEAD_DIM ** (-0.5)
    grad_top = grad_low.astype(jnp.float32)
    grad_down = fold(block_grads(hidden, [grad_low], own, ctx_count), 1)
    grad_hidden_rows = matmul(grad_low, w_down.T)
    grad_up_low = (grad_hidden_rows * gate_pre * logistic).astype(jnp.bfloat16)
    grad_gate_low = (
        grad_hidden_rows * up_pre * (logistic * (1.0 + gate_pre * (1.0 - logistic)))
    ).astype(jnp.bfloat16)
    grad_gate = block_grads(ffn_input, [grad_gate_low], own, ctx_count)
    grad_upw = block_grads(ffn_input, [grad_up_low], own, ctx_count)
    grad_normed_terms = matmul(grad_gate_low, w_gate.T) + matmul(grad_up_low, w_up.T)
    grad_normed_terms = tie(grad_normed_terms, grad_down, grad_gate, grad_upw)
    grad_down = fold_rest(grad_down)
    grad_gate = fold(grad_gate, 1)
    grad_upw = fold(grad_upw, 1)
    grad_ffn = jnp.sum(flatten(grad_normed_terms * middle * second_scale), 0)
    weighted2 = ffn_gain.astype(jnp.float32) * grad_normed_terms
    grad_middle = (
        grad_top
        + second_scale * weighted2
        - middle * second_scale**3 * jnp.mean(weighted2 * middle, -1, keepdims=True)
    )
    branch_low = grad_middle.astype(jnp.bfloat16)
    grad_output = block_grads(attended, [branch_low], own, ctx_count)
    grad_attended = matmul(branch_low, w_output.T).astype(jnp.bfloat16)
    grad_attended = tie(grad_attended, grad_gate, grad_upw, grad_output)
    grad_gate = fold_rest(grad_gate)
    grad_output = fold(grad_output, 1)
    grad_heads = grad_attended.reshape(seq_count, part_len, KV_HEADS, group_size, HEAD_DIM)
    grad_probs = jnp.einsum(
        "bikhd,bjkd->bkhij", grad_heads, value_heads, preferred_element_type=jnp.float32
    )
    grad_scores = (
        soft_weights * (grad_probs - jnp.sum(soft_weights * grad_probs, -1, keepdims=True))
    ).astype(jnp.bfloat16)
    grad_scores = tie(grad_scores, grad_down, grad_output)
    own_dp = lax.axis_index("dp")
    down_owned = scatter_rows(grad_down, own_dp, jnp.bfloat16)
    grad_queries = (
        jnp.einsum("bkhij,bjkd->bikhd", grad_scores, key_heads, preferred_element_type=jnp.float32)
        * score_scale
    )
    grad_keys = (
        jnp.einsum(
            "bkhij,bikhd->bjkd", grad_scores, query_heads, preferred_element_type=jnp.float32
        )
        * score_scale
    )
    grad_values = jnp.einsum(
        "bkhij,bikhd->bjkd", weights_low, grad_heads, preferred_element_type=jnp.float32
    )
    own_keys = grad_keys
    own_values = grad_values.reshape(seq_count, length, kv_width)
    query_low = (
        unrotate(grad_queries.reshape(seq_count, part_len, HEADS, HEAD_DIM), cosine, sine_part)
        .reshape(seq_count, part_len, model_width)
        .astype(jnp.bfloat16)
    )
    key_low = (
        unrotate(own_keys.reshape(seq_count, part_len, KV_HEADS, HEAD_DIM), cosine, sine_part)
        .reshape(seq_count, part_len, kv_width)
        .astype(jnp.bfloat16)
    )
    value_low = own_values.astype(jnp.bfloat16)
    normed = tie(normed, grad_gate)
    gate_owned = scatter_rows(grad_gate, own_dp, jnp.bfloat16)
    up_owned = scatter_rows(fold_rest(grad_upw), own_dp, jnp.bfloat16)
    output_owned = scatter_rows(fold_rest(grad_output), own_dp, jnp.bfloat16)
    grad_qkv = block_grads(normed, [query_low, key_low, value_low], own, ctx_count)
    grad_normed = (
        matmul(query_low, w_query.T) + matmul(key_low, w_key.T) + matmul(value_low, w_value.T)
    )
    grad_attn = jnp.sum(flatten(grad_normed * residual * first_scale), 0)
    weighted1 = attn_gain.astype(jnp.float32) * grad_normed
    grad_input = (
        grad_middle
        + first_scale * weighted1
        - residual * first_scale**3 * jnp.mean(weighted1 * residual, -1, keepdims=True)
    )
    return (
        grad_input,
        (
            grad_attn,
            grad_qkv,
            output_owned,
            grad_ffn,
            gate_owned,
            up_owned,
            down_owned,
        ),
    )


def body(
    inputs,
    positions,
    cotangent,
    attn_gain,
    w_query,
    w_key,
    w_value,
    w_output,
    ffn_gain,
    w_gate,
    w_up,
    w_down,
):
    own = lax.axis_index("ctx")
    own_dp = lax.axis_index("dp")
    ctx_count = lax.axis_size("ctx")
    assert inputs.shape[0] == ctx_count
    q_width, k_width, o_width = w_query.shape[1], w_key.shape[1], w_output.shape[1]

    attn_pack = jnp.concatenate([w_query, w_key, w_value, w_output], 1)
    attn_rows, attn_first = gather_rows(attn_pack, own_dp)
    gains = gather_rows(jnp.stack([attn_gain, ffn_gain], 1), own_dp)[0]
    tokens = to_sequences(inputs, own)
    places = to_sequences(positions, own)
    gate_rows, _ = gather_rows(tie(w_gate, attn_first), own_dp)
    attn_blocks, attn_far = gather_blocks(attn_rows, own)
    up_rows, _ = gather_rows(tie(w_up, attn_far), own_dp)
    gate_blocks, gate_far = gather_blocks(tie(gate_rows, attn_far), own)
    down_rows, _ = gather_rows(tie(w_down, gate_far), own_dp)
    up_blocks, up_far = gather_blocks(tie(up_rows, gate_far), own)
    down_blocks, _ = gather_blocks(tie(down_rows, up_far), own)
    grad_low = to_sequences(tie(cotangent, up_far), own)

    def columns(start, width):
        return jnp.concatenate([block[:, start : start + width] for block in attn_blocks], 1)

    weights = (
        gains[:, 0],
        columns(0, q_width),
        columns(q_width, k_width),
        columns(q_width + k_width, k_width),
        columns(q_width + 2 * k_width, o_width),
        gains[:, 1],
        jnp.concatenate(gate_blocks, 1),
        jnp.concatenate(up_blocks, 1),
        jnp.concatenate(down_blocks, 1),
    )
    result, stored = forward(weights, tokens, places)
    outputs = from_sequences(result, own)
    grad_input, terms = backward(weights, stored, grad_low, own, ctx_count)
    grad_attn, grad_qkv, output_owned, grad_ffn, gate_owned, up_owned, down_owned = terms
    low = jnp.bfloat16
    qkv_owned = scatter_rows(fold_rest(grad_qkv), own_dp, low)
    gain_terms = jnp.stack([grad_attn, grad_ffn], 1)
    for bit in bits_of(ctx_count):
        gain_terms = gain_terms + swap(gain_terms, "ctx", bit)
    gain_owned = scatter_rows(gain_terms, own_dp, jnp.float32)
    input_grad = from_sequences(grad_input.astype(low), own).astype(jnp.float32)
    return (
        outputs,
        input_grad,
        gain_owned[:, 0],
        qkv_owned[:, :q_width],
        qkv_owned[:, q_width : q_width + k_width],
        qkv_owned[:, q_width + k_width :],
        output_owned,
        gain_owned[:, 1],
        gate_owned,
        up_owned,
        down_owned,
    )


def solution(mesh):
    return jax.shard_map(
        body,
        mesh=mesh,
        in_specs=(
            P(None, "dp", "ctx", None),
            P(None, "dp", "ctx"),
            P(None, "dp", "ctx", None),
            P("dp"),
            P("dp", "ctx"),
            P("dp", "ctx"),
            P("dp", "ctx"),
            P("dp", "ctx"),
            P("dp"),
            P("dp", "ctx"),
            P("dp", "ctx"),
            P("dp", "ctx"),
        ),
        out_specs=(
            P(None, "dp", "ctx", None),
            P(None, "dp", "ctx", None),
            P("dp"),
            P("dp", "ctx"),
            P("dp", "ctx"),
            P("dp", "ctx"),
            P("dp", "ctx"),
            P("dp"),
            P("dp", "ctx"),
            P("dp", "ctx"),
            P("dp", "ctx"),
        ),
        check_vma=False,
    )
```

```python
import jax
import jax.numpy as jnp
from jax import lax
from jax.sharding import PartitionSpec as P

HEADS = 15
KV_HEADS = 5
HEAD_DIM = 64


EPS = 1e-05


def turn_tables(places, head_width):
    half_width = head_width // 2
    frequency = 10000.0 ** (-(jnp.arange(half_width, dtype=jnp.float32) * (2.0 / head_width)))
    angles = places.astype(jnp.float32)[..., None] * frequency
    return (jnp.cos(angles)[..., None, :], jnp.sin(angles)[..., None, :])


def rotate(vectors, cosine, sine_part):
    half_width = vectors.shape[-1] // 2
    first_half = vectors[..., :half_width]
    second_half = vectors[..., half_width:]
    return jnp.concatenate(
        [
            first_half * cosine - second_half * sine_part,
            second_half * cosine + first_half * sine_part,
        ],
        axis=-1,
    )


def unrotate(vectors, cosine, sine_part):
    half_width = vectors.shape[-1] // 2
    first_half = vectors[..., :half_width]
    second_half = vectors[..., half_width:]
    return jnp.concatenate(
        [
            first_half * cosine + second_half * sine_part,
            second_half * cosine - first_half * sine_part,
        ],
        axis=-1,
    )


def matmul(left, right):
    return jnp.dot(left, right, preferred_element_type=jnp.float32)


def flatten(values_in):
    return values_in.reshape(-1, values_in.shape[-1])


def swap(value, axis, bit):
    count = lax.axis_size(axis)
    return lax.ppermute(value, axis, [(i, i ^ bit) for i in range(count)])


def tie(value, *earlier):
    return lax.optimization_barrier((value, earlier))[0]


def bits_of(count):
    bits, bit = [], 1
    while bit < count:
        bits.append(bit)
        bit *= 2
    return bits


def in_order(pieces, own, order):
    stacked = jnp.stack(pieces)
    places = [0] * len(order)
    for place, distance in enumerate(order):
        places[distance] = place
    table = jnp.array(places, jnp.int32)
    return [
        lax.dynamic_index_in_dim(stacked, table[own ^ i], 0, keepdims=False)
        for i in range(len(order))
    ]


def gather_rows(shard, own):
    order = [0]
    held = shard[None]
    early = held
    for bit in reversed(bits_of(lax.axis_size("dp"))):
        early = held
        held = jnp.concatenate([held, swap(held, "dp", bit)], 0)
        order = order + [distance ^ bit for distance in order]
    places = [0] * len(order)
    for place, distance in enumerate(order):
        places[distance] = place
    table = jnp.array(places, jnp.int32)
    return jnp.concatenate(
        [
            lax.dynamic_index_in_dim(held, table[own ^ i], 0, keepdims=False)
            for i in range(len(order))
        ],
        0,
    ), early


def gather_blocks(block, own):
    order, held = [0], [block]
    for bit in reversed(bits_of(lax.axis_size("ctx"))):
        held = held + [swap(piece, "ctx", bit) for piece in held]
        order = order + [distance ^ bit for distance in order]
    return in_order(held, own, order), held[1]


def block_grads(left, rights, own, ctx_count):
    blocks = []
    for right in rights:
        flat = flatten(right)
        width = flat.shape[1] // ctx_count
        blocks.append([flat[:, i * width : (i + 1) * width] for i in range(ctx_count)])
    stacked = jnp.stack([jnp.concatenate(parts, 1) for parts in zip(*blocks)])
    rows = flatten(left).T
    return [
        matmul(rows, lax.dynamic_index_in_dim(stacked, own ^ j, 0, keepdims=False)).astype(
            jnp.bfloat16
        )
        for j in range(ctx_count)
    ]


def add(left, right):
    return left.astype(jnp.float32) + right.astype(jnp.float32)


def fold(blocks, bit):
    arrived = [swap(block, "ctx", bit) for block in blocks[1::2]]
    return [
        add(left, right).astype(jnp.bfloat16) for left, right in zip(blocks[0::2], arrived)
    ]


def fold_rest(blocks):
    count = lax.axis_size("ctx")
    bit = count // len(blocks)
    while bit < count:
        blocks = fold(blocks, bit)
        bit *= 2
    return blocks[0]


def rows_by_distance(total, own_dp, wire):
    count = lax.axis_size("dp")
    order = [0]
    for bit in reversed(bits_of(count)):
        order = order + [distance ^ bit for distance in order]
    by_owner = total.reshape(count, total.shape[0] // count, *total.shape[1:]).astype(wire)
    return jnp.stack(
        [lax.dynamic_index_in_dim(by_owner, own_dp ^ k, 0, keepdims=False) for k in order]
    )


def halve(held, bit, wire):
    half = held.shape[0] // 2
    return add(held[:half], swap(held[half:].astype(wire), "dp", bit))


def halve_rest(held, wire):
    count = lax.axis_size("dp")
    bit = count // held.shape[0]
    while bit < count:
        held = halve(held, bit, wire)
        bit *= 2
    return held[0]


def scatter_rows(total, own_dp, wire):
    return halve_rest(rows_by_distance(total, own_dp, wire), wire)


def to_sequences(parts, own):
    count = lax.axis_size("ctx")
    pieces = [lax.dynamic_index_in_dim(parts, own ^ j, 0, keepdims=False) for j in range(count)]
    got = [pieces[0]] + [swap(pieces[j], "ctx", j) for j in range(1, count)]
    return jnp.concatenate(in_order(got, own, list(range(count))), 1)


def from_sequences(whole, own):
    count = lax.axis_size("ctx")
    part = whole.shape[1] // count
    pieces = [
        lax.dynamic_slice_in_dim(whole, (own ^ j) * part, part, 1) for j in range(count)
    ]
    got = [pieces[0]] + [swap(pieces[j], "ctx", j) for j in range(1, count)]
    return jnp.stack(in_order(got, own, list(range(count))))


def forward(weights, tokens, places):
    attn_gain, w_query, w_key, w_value, w_output, ffn_gain, w_gate, w_up, w_down = weights
    seq_count, part_len, model_width = tokens.shape
    group_size = HEADS // KV_HEADS
    score_scale = HEAD_DIM ** (-0.5)
    residual = tokens.astype(jnp.float32)
    first_scale = lax.rsqrt(jnp.mean(residual * residual, -1, keepdims=True) + EPS)
    normed = (residual * first_scale * attn_gain.astype(jnp.float32)).astype(jnp.bfloat16)
    cosine, sine_part = turn_tables(places, HEAD_DIM)
    queries = rotate(
        matmul(normed, w_query).reshape(seq_count, part_len, HEADS, HEAD_DIM), cosine, sine_part
    ).astype(jnp.bfloat16)
    keys_low = rotate(
        matmul(normed, w_key).reshape(seq_count, part_len, KV_HEADS, HEAD_DIM), cosine, sine_part
    ).astype(jnp.bfloat16)
    keys_low = keys_low.reshape(seq_count, part_len, KV_HEADS * HEAD_DIM)
    values_low = matmul(normed, w_value).astype(jnp.bfloat16)
    all_keys, all_values = keys_low, values_low
    length = all_keys.shape[1]
    key_heads = all_keys.reshape(seq_count, length, KV_HEADS, HEAD_DIM)
    value_heads = all_values.reshape(seq_count, length, KV_HEADS, HEAD_DIM)
    query_heads = queries.reshape(seq_count, part_len, KV_HEADS, group_size, HEAD_DIM)
    scores = (
        jnp.einsum("bikhd,bjkd->bkhij", query_heads, key_heads, preferred_element_type=jnp.float32)
        * score_scale
    )
    row_index = jnp.arange(part_len, dtype=jnp.int32)
    starts = row_index[None, :] - places
    col_index = jnp.arange(length, dtype=jnp.int32)
    allowed = (col_index[None, None, :] <= row_index[None, :, None]) & (
        col_index[None, None, :] >= starts[:, :, None]
    )
    scores = jnp.where(allowed[:, None, None], scores, -1e30)
    row_max = jnp.max(scores, -1, keepdims=True)
    exponent = jnp.exp(scores - row_max)
    soft_weights = exponent / jnp.sum(exponent, -1, keepdims=True)
    weights_low = soft_weights.astype(jnp.bfloat16)
    attended = jnp.einsum(
        "bkhij,bjkd->bikhd", weights_low, value_heads, preferred_element_type=jnp.float32
    )
    attended = attended.reshape(seq_count, part_len, model_width).astype(jnp.bfloat16)
    middle = residual + matmul(attended, w_output)
    second_scale = lax.rsqrt(jnp.mean(middle * middle, -1, keepdims=True) + EPS)
    normed2 = (middle * second_scale * ffn_gain.astype(jnp.float32)).astype(jnp.bfloat16)
    gate_pre = matmul(normed2, w_gate)
    up_pre = matmul(normed2, w_up)
    logistic = jax.nn.sigmoid(gate_pre)
    hidden_local = (gate_pre * logistic * up_pre).astype(jnp.bfloat16)
    result = (middle + matmul(hidden_local, w_down)).astype(jnp.bfloat16)
    stored = (
        residual,
        first_scale,
        normed,
        cosine,
        sine_part,
        query_heads,
        key_heads,
        value_heads,
        soft_weights,
        weights_low,
        attended,
        middle,
        second_scale,
        normed2,
        gate_pre,
        up_pre,
        logistic,
        hidden_local,
    )
    return (result, stored)


def backward(weights, stored, grad_low, own, ctx_count):
    attn_gain, w_query, w_key, w_value, w_output, ffn_gain, w_gate, w_up, w_down = weights
    (
        residual,
        first_scale,
        normed,
        cosine,
        sine_part,
        query_heads,
        key_heads,
        value_heads,
        soft_weights,
        weights_low,
        attended,
        middle,
        second_scale,
        ffn_input,
        gate_pre,
        up_pre,
        logistic,
        hidden,
    ) = stored
    seq_count, part_len, model_width = residual.shape
    length = key_heads.shape[1]
    kv_width = KV_HEADS * HEAD_DIM
    group_size = HEADS // KV_HEADS
    score_scale = HEAD_DIM ** (-0.5)
    grad_top = grad_low.astype(jnp.float32)
    grad_down = fold(block_grads(hidden, [grad_low], own, ctx_count), 1)
    grad_hidden_rows = matmul(grad_low, w_down.T)
    grad_up_low = (grad_hidden_rows * gate_pre * logistic).astype(jnp.bfloat16)
    grad_gate_low = (
        grad_hidden_rows * up_pre * (logistic * (1.0 + gate_pre * (1.0 - logistic)))
    ).astype(jnp.bfloat16)
    grad_gate = block_grads(ffn_input, [grad_gate_low], own, ctx_count)
    grad_upw = block_grads(ffn_input, [grad_up_low], own, ctx_count)
    grad_normed_terms = matmul(grad_gate_low, w_gate.T) + matmul(grad_up_low, w_up.T)
    grad_normed_terms = tie(grad_normed_terms, grad_down, grad_gate, grad_upw)
    grad_down = fold_rest(grad_down)
    grad_gate = fold(grad_gate, 1)
    grad_upw = fold(grad_upw, 1)
    grad_ffn = jnp.sum(flatten(grad_normed_terms * middle * second_scale), 0)
    weighted2 = ffn_gain.astype(jnp.float32) * grad_normed_terms
    grad_middle = (
        grad_top
        + second_scale * weighted2
        - middle * second_scale**3 * jnp.mean(weighted2 * middle, -1, keepdims=True)
    )
    branch_low = grad_middle.astype(jnp.bfloat16)
    grad_output = block_grads(attended, [branch_low], own, ctx_count)
    grad_attended = matmul(branch_low, w_output.T).astype(jnp.bfloat16)
    grad_attended = tie(grad_attended, grad_gate, grad_upw, grad_output)
    low, own_dp = jnp.bfloat16, lax.axis_index("dp")
    grad_gate = fold_rest(grad_gate)
    grad_upw = fold_rest(grad_upw)
    grad_output = fold(grad_output, 1)
    down_part = halve(rows_by_distance(grad_down, own_dp, low), 1, low).astype(low)
    grad_heads = grad_attended.reshape(seq_count, part_len, KV_HEADS, group_size, HEAD_DIM)
    grad_probs = jnp.einsum(
        "bikhd,bjkd->bkhij", grad_heads, value_heads, preferred_element_type=jnp.float32
    )
    grad_scores = (
        soft_weights * (grad_probs - jnp.sum(soft_weights * grad_probs, -1, keepdims=True))
    ).astype(jnp.bfloat16)
    gate_part = halve(rows_by_distance(grad_gate, own_dp, low), 1, low).astype(low)
    up_part = halve(rows_by_distance(grad_upw, own_dp, low), 1, low).astype(low)
    grad_scores = tie(grad_scores, down_part, grad_output, grad_gate)
    down_owned = halve_rest(down_part, low)
    grad_output = fold_rest(grad_output)
    grad_queries = (
        jnp.einsum("bkhij,bjkd->bikhd", grad_scores, key_heads, preferred_element_type=jnp.float32)
        * score_scale
    )
    grad_keys = (
        jnp.einsum(
            "bkhij,bikhd->bjkd", grad_scores, query_heads, preferred_element_type=jnp.float32
        )
        * score_scale
    )
    grad_values = jnp.einsum(
        "bkhij,bikhd->bjkd", weights_low, grad_heads, preferred_element_type=jnp.float32
    )
    own_keys = grad_keys
    own_values = grad_values.reshape(seq_count, length, kv_width)
    query_low = (
        unrotate(grad_queries.reshape(seq_count, part_len, HEADS, HEAD_DIM), cosine, sine_part)
        .reshape(seq_count, part_len, model_width)
        .astype(jnp.bfloat16)
    )
    key_low = (
        unrotate(own_keys.reshape(seq_count, part_len, KV_HEADS, HEAD_DIM), cosine, sine_part)
        .reshape(seq_count, part_len, kv_width)
        .astype(jnp.bfloat16)
    )
    value_low = own_values.astype(jnp.bfloat16)
    normed = tie(normed, gate_part, up_part, down_owned, grad_output)
    gate_owned = halve_rest(gate_part, low)
    up_owned = halve_rest(up_part, low)
    output_owned = scatter_rows(grad_output, own_dp, low)
    grad_qkv = block_grads(normed, [query_low, key_low, value_low], own, ctx_count)
    grad_normed = (
        matmul(query_low, w_query.T) + matmul(key_low, w_key.T) + matmul(value_low, w_value.T)
    )
    grad_attn = jnp.sum(flatten(grad_normed * residual * first_scale), 0)
    weighted1 = attn_gain.astype(jnp.float32) * grad_normed
    grad_input = (
        grad_middle
        + first_scale * weighted1
        - residual * first_scale**3 * jnp.mean(weighted1 * residual, -1, keepdims=True)
    )
    return (
        grad_input,
        (
            grad_attn,
            grad_qkv,
            output_owned,
            grad_ffn,
            gate_owned,
            up_owned,
            down_owned,
        ),
    )


def body(
    inputs,
    positions,
    cotangent,
    attn_gain,
    w_query,
    w_key,
    w_value,
    w_output,
    ffn_gain,
    w_gate,
    w_up,
    w_down,
):
    own = lax.axis_index("ctx")
    own_dp = lax.axis_index("dp")
    ctx_count = lax.axis_size("ctx")
    assert inputs.shape[0] == ctx_count
    q_width, k_width, o_width = w_query.shape[1], w_key.shape[1], w_output.shape[1]

    attn_pack = jnp.concatenate([w_query, w_key, w_value, w_output], 1)
    attn_rows, attn_early = gather_rows(attn_pack, own_dp)
    gains = gather_rows(jnp.stack([attn_gain, ffn_gain], 1), own_dp)[0]
    tokens = to_sequences(inputs, own)
    places = to_sequences(positions, own)
    w_gate, w_up, w_down = tie((w_gate, w_up, w_down), attn_early)
    gate_rows, up_rows, down_rows = [gather_rows(w, own_dp)[0] for w in (w_gate, w_up, w_down)]
    attn_blocks, attn_far = gather_blocks(attn_rows, own)
    gate_rows, up_rows, down_rows = tie((gate_rows, up_rows, down_rows), attn_far)
    gate_blocks = gather_blocks(gate_rows, own)[0]
    up_blocks = gather_blocks(up_rows, own)[0]
    down_blocks = gather_blocks(down_rows, own)[0]
    grad_low = to_sequences(tie(cotangent, attn_rows), own)

    def columns(start, width):
        return jnp.concatenate([block[:, start : start + width] for block in attn_blocks], 1)

    weights = (
        gains[:, 0],
        columns(0, q_width),
        columns(q_width, k_width),
        columns(q_width + k_width, k_width),
        columns(q_width + 2 * k_width, o_width),
        gains[:, 1],
        jnp.concatenate(gate_blocks, 1),
        jnp.concatenate(up_blocks, 1),
        jnp.concatenate(down_blocks, 1),
    )
    result, stored = forward(weights, tokens, places)
    outputs = from_sequences(result, own)
    grad_input, terms = backward(weights, stored, grad_low, own, ctx_count)
    grad_attn, grad_qkv, output_owned, grad_ffn, gate_owned, up_owned, down_owned = terms
    low = jnp.bfloat16
    qkv_owned = scatter_rows(fold_rest(grad_qkv), own_dp, low)
    gain_terms = jnp.stack([grad_attn, grad_ffn], 1)
    for bit in bits_of(ctx_count):
        gain_terms = gain_terms + swap(gain_terms, "ctx", bit)
    gain_owned = scatter_rows(gain_terms, own_dp, jnp.float32)
    input_grad = from_sequences(grad_input.astype(low), own).astype(jnp.float32)
    return (
        outputs,
        input_grad,
        gain_owned[:, 0],
        qkv_owned[:, :q_width],
        qkv_owned[:, q_width : q_width + k_width],
        qkv_owned[:, q_width + k_width :],
        output_owned,
        gain_owned[:, 1],
        gate_owned,
        up_owned,
        down_owned,
    )


def solution(mesh):
    return jax.shard_map(
        body,
        mesh=mesh,
        in_specs=(
            P(None, "dp", "ctx", None),
            P(None, "dp", "ctx"),
            P(None, "dp", "ctx", None),
            P("dp"),
            P("dp", "ctx"),
            P("dp", "ctx"),
            P("dp", "ctx"),
            P("dp", "ctx"),
            P("dp"),
            P("dp", "ctx"),
            P("dp", "ctx"),
            P("dp", "ctx"),
        ),
        out_specs=(
            P(None, "dp", "ctx", None),
            P(None, "dp", "ctx", None),
            P("dp"),
            P("dp", "ctx"),
            P("dp", "ctx"),
            P("dp", "ctx"),
            P("dp", "ctx"),
            P("dp"),
            P("dp", "ctx"),
            P("dp", "ctx"),
            P("dp", "ctx"),
        ),
        check_vma=False,
    )
```
